32 devices in a mesh: out: 4 (over y, x), inp: 8 (over z, core).
Axes of the slice: x: 2, y: 2, z: 4, core: 2. Of those that a mesh axis runs over, the one named last changes fastest.
Arguments:
- grads: bfloat16 [512, 28672], P('out', 'inp'), may hold values from -1.1953125 to 1.1953125
- acts: bfloat16 [512, 8192], P('inp', 'out'), may hold values from -6 to 6
- basis_out: bfloat16 [28672, 14336], P('inp', 'out'), may hold values from -0.03125 to 0.03125
- basis_in: bfloat16 [8192, 8192], P('out', 'inp'), may hold values from -0.0625 to 0.0625
- old_correction: float32 [14336, 8192], P('out', 'inp'), may hold values from 0.1 to 2
- lengths: int32 [4], replicated, may hold values from 1 to 256, 512 in all
Outputs:
- correction: float32 [14336, 8192], P('out', 'inp')
The draws below stay inside these ranges and needn't reach their ends.
Inputs may be any that keep to these rules, and one draw needn't show every extreme that they name: The lengths sum to 512; the longest example has exactly 256 tokens.
All inputs are finite; a program needn't handle non-finite values.
Results may differ from the reference program's by a relative error of at most 0.0021.
Values may be sent and summed in bfloat16 or wider, within the bound.
A program may use at most 128 MiB of HBM per device.

```python
import math
import jax
import jax.numpy as jnp
import numpy as np
from jax import lax

DOUT = 28672
DIN = 8192
KG = 14336
TOKENS = 512
EX = 4
CAP = 256


def spiked(entries, key, source, target, blocks, factor):
    def block_of(axis_at):
        return (jnp.arange(entries.shape[axis_at]) // (entries.shape[axis_at] // blocks)).reshape((-1,) + (1,) * (entries.ndim - 1 - axis_at))

    near = jax.random.permutation(key, blocks)[block_of(target)]
    far = (block_of(target) + blocks // 2) % blocks
    return jnp.where((block_of(source) == near) | (block_of(source) == far), factor * entries, entries)


def levels(own_key, dims, split, least, largest):
    loudness = 1.0
    for dim, parts in split:
        heights = jax.random.uniform(jax.random.fold_in(jax.random.fold_in(own_key, 6), dim), (parts,), jnp.float32, least / len(split), largest / len(split))
        loudness = loudness * jnp.repeat(jnp.exp(heights), dims[dim] // parts).reshape((-1,) + (1,) * (len(dims) - 1 - dim))
    return loudness


def profile(amount, total, most, slope):
    loads = [(1 << 20) // math.isqrt(rank ** slope) + 1 for rank in range(2, amount + 1)]
    rest, holding = total - most - (amount - 1), [1] * (amount - 1)
    while rest > 0:
        candidates = [i for i in range(amount - 1) if holding[i] < most]
        pool, remaining = sum([loads[i] for i in candidates]), rest
        for i in candidates:
            extra = min(most - holding[i], max(1, remaining * loads[i] // pool), rest)
            holding[i] = holding[i] + extra
            rest = rest - extra
    return np.array([most] + holding)


def uneven_parts(rng, count, total, limit, lean):
    if count == 2:
        one = jax.random.randint(rng, (), max(1, total - limit), min(limit, total - 1) + 1)
        return jnp.stack([one, total - one])
    sizes = jnp.asarray(profile(count, total, limit, lean), jnp.int32)
    couples = (count - 1) // 2
    source_of, taker = sizes[1:1 + 2 * couples:2], sizes[2:2 + 2 * couples:2]
    margin = jnp.minimum(source_of - 1, limit - taker)
    shifted = jax.random.randint(jax.random.fold_in(rng, 1), (couples,), 0, 1 << 20) % (margin + 1)
    sizes = sizes.at[1:1 + 2 * couples:2].set(source_of - shifted).at[2:2 + 2 * couples:2].set(taker + shifted)
    return sizes[jax.random.permutation(jax.random.fold_in(rng, 2), count)]


def gaussian(rng, shape, scale, bound, shards=(), kind=jnp.bfloat16):
    level = levels(rng, shape, shards, -0.22, 0.18) if shards else 1.0
    result = jax.random.normal(rng, shape, jnp.float32) * scale * level
    return jnp.minimum(jnp.maximum(result, -bound), bound).astype(kind)


def bell_draw_with(key, shape, width, bound, cuts, heavy, kind=jnp.bfloat16):
    result = width * jax.random.normal(key, shape, jnp.float32)
    if cuts:
        result = result * levels(key, shape, cuts, -0.22, 0.18)
    return jnp.clip(spiked(result, jax.random.fold_in(key, 3), *heavy), -bound, bound).astype(kind)


def setup_inputs(seed: int = 0) -> dict:
    arg_keys = jax.random.split(jax.random.key(seed), 7)
    grads = bell_draw_with(arg_keys[0], (TOKENS, DOUT), 0.2, 1.1953125, ((0, 4), (1, 8)), (1, 0, 8, 2.0))
    acts = bell_draw_with(arg_keys[1], (TOKENS, DIN), 1.0, 6.0, ((0, 8), (1, 4)), (1, 0, 8, 2.0))
    basis_out = gaussian(arg_keys[2], (DOUT, KG), DOUT ** -0.5, 0.03125, ((0, 8), (1, 4)))
    basis_in = gaussian(arg_keys[3], (DIN, DIN), DIN ** -0.5, 0.0625, ((0, 4), (1, 8)))
    old_correction = jnp.clip(jnp.exp(math.log(2.0) - 2.9957323 * jax.random.uniform(arg_keys[4], (KG, DIN), jnp.float32) ** levels(arg_keys[4], (KG, DIN), ((0, 4), (1, 8)), -0.2, 0.2)), 0.1, 2.0)
    lengths = uneven_parts(arg_keys[5], EX, TOKENS, CAP, 2).astype(jnp.int32)
    return dict(grads=grads, acts=acts, basis_out=basis_out, basis_in=basis_in, old_correction=old_correction, lengths=lengths)


def reference(grads, acts, basis_out, basis_in, old_correction, lengths):
    grad_rot = jnp.dot(grads, basis_out, preferred_element_type=jnp.float32).astype(jnp.bfloat16)
    act_rot = jnp.dot(acts, basis_in, preferred_element_type=jnp.float32).astype(jnp.bfloat16)
    offsets = (jnp.cumsum(lengths) - lengths).astype(jnp.int32)
    row_count = grads.shape[0]

    def add_example(example, running):
        offset = offsets[example]
        length = lengths[example]
        first_row = jnp.minimum(offset, row_count - CAP).astype(jnp.int32)
        places = first_row + jnp.arange(CAP, dtype=jnp.int32)
        inside = (places >= offset) & (places < offset + length)
        grad_block = lax.dynamic_slice_in_dim(grad_rot, first_row, CAP, 0)
        act_block = lax.dynamic_slice_in_dim(act_rot, first_row, CAP, 0)
        act_block = jnp.where(inside[:, None], act_block, jnp.zeros((), act_block.dtype))
        projected = lax.dot_general(grad_block, act_block, (((0,), (0,)), ((), ())), preferred_element_type=jnp.float32)
        return running + projected * projected

    running = lax.fori_loop(0, EX, add_example, jnp.zeros(old_correction.shape, jnp.float32))
    return 0.8 * old_correction + 0.2 * running / EX
```

```python
import functools

import jax
import jax.numpy as jnp
from jax import lax
from jax.experimental import pallas as pl
from jax.experimental.pallas import tpu as pltpu
from jax.sharding import PartitionSpec as P

CAP = 256
GRADS_MAX, ACTS_MAX = 1.1953125, 6.0
BASIS_OUT_MAX, BASIS_IN_MAX = 0.03125, 0.0625
MESH = pl.DeviceIdType.MESH
LAG = 2
TILE = 256
HALF = TILE // 2
WIRE = jnp.int16
LEVELS = 32767.0


def encode(value, bound):
    level = jnp.sqrt(jnp.sqrt(jnp.abs(value) * (1.0 / bound))) * LEVELS + 0.5
    level = jnp.minimum(level, LEVELS).astype(jnp.int32)
    return jnp.where(value < 0, -level, level).astype(WIRE)


def decode(level, bound):
    root = level.astype(jnp.int32).astype(jnp.float32) * (1.0 / LEVELS)
    return (root * root) * (root * jnp.abs(root)) * bound


def rotate_kernel(
    nz,
    g_bound,
    a_bound,
    grads,
    acts,
    basis_out,
    basis_in,
    res,
    act_res,
    gall,
    bout,
    bin_,
    own,
    psend,
    precv,
    rsend,
    rrecv,
    aall,
    apart,
    asend,
    arecv1,
    arecv2,
    load_sem,
    basis_sem,
    g_sem,
    p_sem,
    r_sem,
    f_sem,
    q_sem,
    az_sem,
    ap_sem,
    ax_sem,
):
    o, i = lax.axis_index("out"), lax.axis_index("inp")
    z, core = i // 2, i % 2
    x, y = o % 2, o // 2
    xo, yo = y * 2 + (1 - x), (1 - y) * 2 + x
    do = (1 - y) * 2 + (1 - x)
    rows = grads.shape[0]
    tiles = basis_out.shape[1] // TILE
    per = tiles // 2
    count = 4 * per
    arows = acts.shape[0]
    right, left = (i + 2) % (2 * nz), (i + 2 * nz - 2) % (2 * nz)
    pair = z * 2 + (1 - core)
    last = nz - 1

    def remote(src, dst, sems, device):
        return pltpu.make_async_remote_copy(
            src_ref=src, dst_ref=dst, send_sem=sems[0], recv_sem=sems[1], device_id=device, device_id_type=MESH
        )

    def basis_copy(n):
        j, mine = n // 2, n % 2
        tile = jnp.where(mine == 1, core, 1 - core) * per + j
        return pltpu.make_async_copy(
            basis_out.at[:, pl.ds(pl.multiple_of(tile * TILE, TILE), TILE)], bout.at[n], basis_sem.at[n]
        )

    own_grads = pltpu.make_async_copy(grads, gall.at[o], load_sem.at[0])
    own_acts = pltpu.make_async_copy(acts, aall.at[i], load_sem.at[1])
    in_basis = pltpu.make_async_copy(basis_in, bin_, load_sem.at[2])
    own_grads.start()
    own_acts.start()
    lax.fori_loop(0, tiles, lambda n, c: (basis_copy(n).start(), c)[1], 0)
    in_basis.start()

    barrier = pltpu.get_barrier_semaphore()
    for device in ((xo, i), (yo, i), (o, pair)):
        pl.semaphore_signal(barrier, inc=1, device_id=device, device_id_type=MESH)

    @pl.when(z > 0)
    def _():
        pl.semaphore_signal(barrier, inc=1, device_id=(o, left), device_id_type=MESH)

    @pl.when(z < last)
    def _():
        pl.semaphore_signal(barrier, inc=1, device_id=(o, right), device_id_type=MESH)

    pl.semaphore_wait(barrier, 3 + (z + nz - 1) // nz + 1 - (z + 1) // nz)

    half = rows // 2

    def g_copy(which, source, lo, size, device):
        part = gall.at[source, pl.ds(lo, size), :]
        src = grads if which < 2 else part
        return remote(src, part, (g_sem.at[which, 0], g_sem.at[which, 1]), device)

    g_x, g_y = g_copy(0, o, 0, rows, (xo, i)), g_copy(1, o, 0, rows, (yo, i))
    g_x_in, g_y_in = g_copy(0, xo, 0, rows, (xo, i)), g_copy(1, yo, 0, rows, (yo, i))
    g_xy, g_yx = g_copy(2, xo, 0, half, (yo, i)), g_copy(3, yo, half, half, (xo, i))
    g_xy_in, g_yx_in = g_copy(2, do, 0, half, (yo, i)), g_copy(3, do, half, half, (xo, i))
    g_x.start()
    g_y.start()

    def az_copy(direction, hop, chip):
        block = aall.at[chip * 2 + core]
        return remote(
            acts if hop == 0 else block,
            block,
            (az_sem.at[direction, hop, 0], az_sem.at[direction, hop, 1]),
            (o, right if direction == 0 else left),
        )

    def ap_copy(chip, at_home):
        block = aall.at[chip * 2 + (core if at_home else 1 - core)]
        return remote(block, block, (ap_sem.at[chip, 0], ap_sem.at[chip, 1]), (o, pair))

    @pl.when(z < last)
    def _():
        az_copy(0, 0, z).start()

    @pl.when(z > 0)
    def _():
        az_copy(1, 0, z).start()

    own_acts.wait()
    ap_copy(z, True).start()
    own_grads.wait()

    def acts_hop(hop):
        @pl.when(z >= hop)
        def _():
            az_copy(0, hop - 1, z - hop).wait_recv()
            if hop < last:
                @pl.when(z < last)
                def _():
                    az_copy(0, hop, z - hop).start()

            ap_copy(z - hop, True).start()

        @pl.when(z + hop <= last)
        def _():
            az_copy(1, hop - 1, z + hop).wait_recv()
            if hop < last:
                @pl.when(z > 0)
                def _():
                    az_copy(1, hop, z + hop).start()

            ap_copy(z + hop, True).start()

    wide = act_res.shape[2] // 2
    first, second = (xo, yo), (yo, xo)

    def quarter(side, keep, n):
        a = x if side == 0 else y
        a = a if keep else 1 - a
        return n * 2 + a if side == 0 else a * 2 + n

    def ax(side, n):
        return ax_sem.at[side, n, 0], ax_sem.at[side, n, 1]

    def ax_first(side, n):
        return remote(
            asend.at[side, quarter(side, False, n)], arecv1.at[side, n], ax(side, n), (first[side], i)
        )

    def ax_second(side):
        q = second[side]
        return remote(asend.at[side, q], arecv2.at[side], ax(side, 2), (q, i))

    def ax_columns(q, side):
        return act_res.at[q, :, pl.ds(side * wide, wide)]

    def ax_back(side, q):
        return remote(ax_columns(q, side), ax_columns(q, side), ax(side, 3), (second[side], i))

    def ax_all(side, n, keep):
        q = quarter(side, keep, n)
        return remote(ax_columns(q, side), ax_columns(q, side), ax(side, 4 + n), (first[side], i))

    def act_product():
        in_basis.wait()
        for chip in range(nz):
            ap_copy(chip, False).wait_recv()
        blocks = aall.shape[0] // 4

        def one(q, carry):
            lhs = aall[pl.ds(q * blocks, blocks)].reshape(blocks * arows, -1)
            for side in range(2):
                value = jnp.dot(
                    lhs, bin_[:, side * wide : (side + 1) * wide], preferred_element_type=jnp.float32
                )
                apart[side, q] = value
                asend[side, q] = encode(value, a_bound)
            return carry

        lax.fori_loop(0, 4, one, 0)
        for side in range(2):
            for n in range(2):
                ax_first(side, n).start()

    def act_second():
        for side in range(2):
            for n in range(2):
                ax_first(side, n).wait_recv()
                q = quarter(side, True, n)
                apart[side, q] = apart[side, q] + decode(arecv1[side, n], a_bound)
            q = second[side]
            asend[side, q] = encode(apart[side, q], a_bound)
            ax_second(side).start()

    def act_third():
        for side in range(2):
            ax_second(side).wait_recv()
            total = apart[side, o] + decode(arecv2[side], a_bound)
            act_res[o, :, side * wide : (side + 1) * wide] = total.astype(jnp.bfloat16)
            ax_back(side, o).start()

    def act_fourth():
        for side in range(2):
            ax_back(side, second[side]).wait_recv()
            for n in range(2):
                ax_all(side, n, True).start()

    def block_of(k):
        b = k // per
        bx, by = b % 2, b // 2
        return (y + by) % 2 * 2 + (x + bx) % 2

    def pair_copy(k):
        return remote(psend.at[k], precv.at[k], (p_sem.at[k, 0], p_sem.at[k, 1]), (o, pair))

    def sum_copy(d, k):
        return remote(
            rsend.at[d, k], rrecv.at[d, k], (r_sem.at[d, k, 0], r_sem.at[d, k, 1]), (o, right if d == 0 else left)
        )

    def place(d, k, of_core):
        return res.at[of_core * per + k % per, block_of(k), :, pl.ds(d * HALF, HALF)]

    def out_copy(d, k):
        ref = place(d, k, core)
        return remote(ref, ref, (f_sem.at[d, k, 0], f_sem.at[d, k, 1]), (o, left if d == 0 else right))

    def share_copy(d, k, of_core):
        ref = place(d, k, of_core)
        return remote(ref, ref, (q_sem.at[d, k, 0], q_sem.at[d, k, 1]), (o, pair))

    def valid(k):
        return (k >= 0) & (k < count)

    def step(t, carry):
        for hop in range(1, nz):
            pl.when(t == 2 * hop)(functools.partial(acts_hop, hop))

        @pl.when(t == per)
        def _():
            g_x_in.wait_recv()
            g_xy.start()
            g_y_in.wait_recv()
            g_yx.start()

        pl.when(t == per + 2)(act_product)

        @pl.when(t == 3 * per)
        def _():
            g_xy_in.wait_recv()
            g_yx_in.wait_recv()

        pl.when(t == 3 * per - 3)(act_second)
        pl.when(t == 3 * per + 3)(act_third)
        pl.when(t == 4 * per)(act_fourth)

        @pl.when(t < count)
        def _():
            j = t % per

            @pl.when(t < per)
            def _():
                basis_copy(2 * j).wait()
                basis_copy(2 * j + 1).wait()

            lhs = gall[block_of(t)]
            psend[t] = encode(jnp.dot(lhs, bout[2 * j], preferred_element_type=jnp.float32), g_bound)
            pair_copy(t).start()
            own[t] = jnp.dot(lhs, bout[2 * j + 1], preferred_element_type=jnp.float32)

        k = t - 1

        @pl.when(valid(k))
        def _():
            pair_copy(k).wait_recv()
            own[k] = own[k] + decode(precv[k], g_bound)

        for d in range(2):
            hops = z if d == 0 else last - z
            k = t - 1 - LAG * hops

            @pl.when(valid(k))
            def _(d=d, hops=hops, k=k):
                cols = slice(d * HALF, (d + 1) * HALF)

                @pl.when(hops > 0)
                def _():
                    sum_copy(d, k).wait_recv()
                    own[k, :, cols] = own[k, :, cols] + decode(rrecv[d, k], g_bound)

                @pl.when(hops < last)
                def _():
                    rsend[d, k] = encode(own[k, :, cols], g_bound)
                    sum_copy(d, k).start()

                @pl.when(hops == last)
                def _():
                    res[core * per + k % per, block_of(k), :, cols] = own[k, :, cols].astype(jnp.bfloat16)
                    out_copy(d, k).start()
                    share_copy(d, k, core).start()

            k2 = t - 1 - LAG * last - LAG * (last - hops)

            @pl.when(valid(k2) & (hops < last))
            def _(d=d, hops=hops, k=k2):
                out_copy(d, k).wait_recv()

                @pl.when(hops > 0)
                def _():
                    out_copy(d, k).start()

                share_copy(d, k, core).start()

        return carry

    lax.fori_loop(0, count + 1 + 2 * LAG * last, step, 0)

    for side in range(2):
        for n in range(2):
            ax_all(side, n, False).wait_recv()
            ax_all(side, n, True).wait_send()
            ax_first(side, n).wait_send()
        ax_second(side).wait_send()
        ax_back(side, o).wait_send()
    for copy in (g_x, g_y, g_xy, g_yx):
        copy.wait_send()
    for chip in range(nz):
        ap_copy(chip, True).wait_send()
    for hop in range(last):
        @pl.when((z < last) & (z >= hop))
        def _(hop=hop):
            az_copy(0, hop, z - hop).wait_send()

        @pl.when((z > 0) & (z + hop <= last))
        def _(hop=hop):
            az_copy(1, hop, z + hop).wait_send()

    def finish(k, carry):
        pair_copy(k).wait_send()
        for d in range(2):
            hops = z if d == 0 else last - z
            share_copy(d, k, 1 - core).wait_recv()
            share_copy(d, k, core).wait_send()

            @pl.when(hops < last)
            def _(d=d):
                sum_copy(d, k).wait_send()

            @pl.when(hops > 0)
            def _(d=d):
                out_copy(d, k).wait_send()

        return carry

    lax.fori_loop(0, count, finish, 0)


def rotate(nz, grads, acts, basis_out, basis_in):
    rows, arows = grads.shape[0], acts.shape[0]
    depth, columns = basis_out.shape
    adepth, acolumns = basis_in.shape
    tiles = columns // TILE
    count = 4 * (tiles // 2)
    wide = acolumns // 2
    blocks = 2 * nz
    g_bound = GRADS_MAX * BASIS_OUT_MAX * depth * blocks * 1.02
    a_bound = ACTS_MAX * BASIS_IN_MAX * adepth * 4 * 1.02
    dma = pltpu.SemaphoreType.DMA
    any_spec = pl.BlockSpec(memory_space=pl.ANY)
    vmem_spec = pl.BlockSpec(memory_space=pltpu.VMEM)
    return pl.pallas_call(
        functools.partial(rotate_kernel, nz, g_bound, a_bound),
        out_shape=(
            jax.ShapeDtypeStruct((tiles, 4, rows, TILE), jnp.bfloat16),
            jax.ShapeDtypeStruct((4, blocks * arows // 4, acolumns), jnp.bfloat16),
        ),
        in_specs=[any_spec] * 4,
        out_specs=(vmem_spec, vmem_spec),
        scratch_shapes=[
            pltpu.VMEM((4, rows, depth), jnp.bfloat16),
            pltpu.VMEM((tiles, depth, TILE), jnp.bfloat16),
            pltpu.VMEM((adepth, acolumns), jnp.bfloat16),
            pltpu.VMEM((count, rows, TILE), jnp.float32),
            pltpu.VMEM((count, rows, TILE), WIRE),
            pltpu.VMEM((count, rows, TILE), WIRE),
            pltpu.VMEM((2, count, rows, HALF), WIRE),
            pltpu.VMEM((2, count, rows, HALF), WIRE),
            pltpu.VMEM((blocks, arows, adepth), jnp.bfloat16),
            pltpu.VMEM((2, 4, rows, wide), jnp.float32),
            pltpu.VMEM((2, 4, rows, wide), WIRE),
            pltpu.VMEM((2, 2, rows, wide), WIRE),
            pltpu.VMEM((2, rows, wide), WIRE),
            dma((3,)),
            dma((tiles,)),
            dma((4, 2)),
            dma((count, 2)),
            dma((2, count, 2)),
            dma((2, count, 2)),
            dma((2, count, 2)),
            dma((2, nz - 1, 2)),
            dma((nz, 2)),
            dma((2, 6, 2)),
        ],
        compiler_params=pltpu.CompilerParams(
            collective_id=0, has_side_effects=True, vmem_limit_bytes=62 * 1024 * 1024
        ),
        name="rotate",
    )(grads, acts, basis_out, basis_in)


def correct_kernel(examples, lengths, grad, act, old, out, turned, running):
    windows = grad.shape[0] // CAP
    for w in range(windows):
        turned[w] = grad[w * CAP : (w + 1) * CAP, :].T
    running[...] = jnp.zeros_like(running)
    rows = lax.broadcasted_iota(jnp.int32, (CAP, 1), 0)

    def add_example(e, offset):
        end = offset + lengths[e]
        w = jnp.minimum(offset // CAP, windows - 1)

        def part(at):
            places = at * CAP + rows
            inside = (places >= offset) & (places < end)
            block = act[pl.ds(pl.multiple_of(at * CAP, CAP), CAP), :]
            block = jnp.where(inside, block, jnp.zeros_like(block))
            return jnp.dot(turned[at], block, preferred_element_type=jnp.float32)

        @pl.when(end <= (w + 1) * CAP)
        def _():
            projected = part(w)
            running[...] += projected * projected

        @pl.when(end > (w + 1) * CAP)
        def _():
            projected = part(w) + part(w + 1)
            running[...] += projected * projected

        return end

    lax.fori_loop(0, examples, add_example, jnp.int32(0))
    out[...] = 0.8 * old[...] + 0.2 * running[...] / examples


def correct(grad, act, old, lengths):
    tiles, tokens, width = grad.shape
    columns = act.shape[1]
    examples = lengths.shape[0]
    return pl.pallas_call(
        functools.partial(correct_kernel, examples),
        out_shape=jax.ShapeDtypeStruct(old.shape, jnp.float32),
        grid_spec=pltpu.PrefetchScalarGridSpec(
            num_scalar_prefetch=1,
            grid=(tiles,),
            in_specs=[
                pl.BlockSpec((None, tokens, width), lambda n, _: (n, 0, 0)),
                pl.BlockSpec((tokens, columns), lambda n, _: (0, 0)),
                pl.BlockSpec((width, columns), lambda n, _: (n, 0)),
            ],
            out_specs=pl.BlockSpec((width, columns), lambda n, _: (n, 0)),
            scratch_shapes=[
                pltpu.VMEM((tokens // CAP, width, CAP), jnp.bfloat16),
                pltpu.VMEM((width, columns), jnp.float32),
            ],
        ),
        compiler_params=pltpu.CompilerParams(vmem_limit_bytes=40 * 1024 * 1024),
        name="correct",
    )(lengths, grad, act, old)


def gather_rotations(grads, acts, basis_out, basis_in):
    gathered = lax.all_gather(grads, "out", axis=0, tiled=True)
    scattered = lax.psum_scatter(
        jnp.dot(gathered, basis_out, preferred_element_type=jnp.float32), "inp", scatter_dimension=0, tiled=True
    )
    grad_rot = lax.all_gather(scattered.astype(jnp.bfloat16), "inp", axis=0, tiled=True)
    gathered_acts = lax.all_gather(acts, "inp", axis=0, tiled=True)
    act_scattered = lax.psum_scatter(
        jnp.dot(gathered_acts, basis_in, preferred_element_type=jnp.float32), "out", scatter_dimension=0, tiled=True
    )
    act_rot = lax.all_gather(act_scattered.astype(jnp.bfloat16), "out", axis=0, tiled=True)
    tokens, columns = grad_rot.shape
    width = min(columns, TILE) if columns % TILE == 0 else HALF
    return grad_rot.reshape(tokens, columns // width, width).transpose(1, 0, 2), act_rot


def body(outs, nz, grads, acts, basis_out, basis_in, old_correction, lengths):
    if outs == 4:
        grad, act = rotate(nz, grads, acts, basis_out, basis_in)
        tiles, blocks, rows, width = grad.shape
        grad = grad.reshape(tiles, blocks * rows, width)
        act = act.reshape(-1, act.shape[-1])
    else:
        grad, act = gather_rotations(grads, acts, basis_out, basis_in)
    return correct(grad, act, old_correction, lengths)


def solution(mesh):
    in_specs = (
        P("out", "inp"),
        P("inp", "out"),
        P("inp", "out"),
        P("out", "inp"),
        P("out", "inp"),
        P(),
    )
    run = functools.partial(body, mesh.shape["out"], mesh.shape["inp"] // 2)
    return jax.shard_map(run, mesh=mesh, in_specs=in_specs, out_specs=P("out", "inp"), check_vma=False)
```

```python
import functools

import jax
import jax.numpy as jnp
from jax import lax
from jax.experimental import pallas as pl
from jax.experimental.pallas import tpu as pltpu
from jax.sharding import PartitionSpec as P

CAP = 256
GRADS_MAX, ACTS_MAX = 1.1953125, 6.0
BASIS_OUT_MAX, BASIS_IN_MAX = 0.03125, 0.0625
MESH = pl.DeviceIdType.MESH
LAG = 2
GAP = 7
TILE = 256
HALF = TILE // 2
WIRE = jnp.int16
LEVELS = 32767.0


def encode(value, bound):
    level = jnp.sqrt(jnp.sqrt(jnp.abs(value) * (1.0 / bound))) * LEVELS + 0.5
    level = jnp.minimum(level, LEVELS).astype(jnp.int32)
    return jnp.where(value < 0, -level, level).astype(WIRE)


def decode(level, bound):
    root = level.astype(jnp.int32).astype(jnp.float32) * (1.0 / LEVELS)
    return (root * root) * (root * jnp.abs(root)) * bound


def rotate_kernel(
    nz,
    g_bound,
    a_bound,
    grads,
    acts,
    basis_out,
    basis_in,
    res,
    act_res,
    gall,
    bout,
    bin_,
    own,
    psend,
    precv,
    rsend,
    rrecv,
    aall,
    apart,
    asend,
    arecv1,
    arecv2,
    load_sem,
    basis_sem,
    g_sem,
    p_sem,
    r_sem,
    f_sem,
    q_sem,
    s_sem,
    az_sem,
    ap_sem,
    ax_sem,
):
    o, i = lax.axis_index("out"), lax.axis_index("inp")
    z, core = i // 2, i % 2
    x, y = o % 2, o // 2
    xo, yo = y * 2 + (1 - x), (1 - y) * 2 + x
    do = (1 - y) * 2 + (1 - x)
    rows = grads.shape[0]
    tiles = basis_out.shape[1] // TILE
    per = tiles // 2
    count = 4 * per
    arows = acts.shape[0]
    right, left = (i + 2) % (2 * nz), (i + 2 * nz - 2) % (2 * nz)
    pair = z * 2 + (1 - core)
    last = nz - 1

    def remote(src, dst, sems, device):
        return pltpu.make_async_remote_copy(
            src_ref=src, dst_ref=dst, send_sem=sems[0], recv_sem=sems[1], device_id=device, device_id_type=MESH
        )

    def basis_copy(n):
        j, mine = n // 2, n % 2
        tile = jnp.where(mine == 1, core, 1 - core) * per + j
        return pltpu.make_async_copy(
            basis_out.at[:, pl.ds(pl.multiple_of(tile * TILE, TILE), TILE)], bout.at[n], basis_sem.at[n]
        )

    own_grads = pltpu.make_async_copy(grads, gall.at[0], load_sem.at[0])
    own_acts = pltpu.make_async_copy(acts, aall.at[i], load_sem.at[1])
    in_basis = pltpu.make_async_copy(basis_in, bin_, load_sem.at[2])
    own_grads.start()
    own_acts.start()
    lax.fori_loop(0, tiles, lambda n, c: (basis_copy(n).start(), c)[1], 0)
    in_basis.start()

    barrier = pltpu.get_barrier_semaphore()
    for device in ((xo, i), (yo, i), (o, pair)):
        pl.semaphore_signal(barrier, inc=1, device_id=device, device_id_type=MESH)

    @pl.when(z > 0)
    def _():
        pl.semaphore_signal(barrier, inc=1, device_id=(o, left), device_id_type=MESH)

    @pl.when(z < last)
    def _():
        pl.semaphore_signal(barrier, inc=1, device_id=(o, right), device_id_type=MESH)

    pl.semaphore_wait(barrier, 3 + (z + nz - 1) // nz + 1 - (z + 1) // nz)

    half = rows // 2

    def g_copy(which, src, slot, lo, size, device):
        part = gall.at[slot, pl.ds(lo, size), :]
        return remote(src, part, (g_sem.at[which, 0], g_sem.at[which, 1]), device)

    g_x, g_y = g_copy(0, grads, 1, 0, rows, (xo, i)), g_copy(1, grads, 2, 0, rows, (yo, i))
    g_xy = g_copy(2, gall.at[1, pl.ds(0, half), :], 3, 0, half, (yo, i))
    g_yx = g_copy(3, gall.at[2, pl.ds(half, half), :], 3, half, half, (xo, i))
    g_x.start()
    g_y.start()

    def az_copy(direction, hop, chip):
        block = aall.at[chip * 2 + core]
        return remote(
            acts if hop == 0 else block,
            block,
            (az_sem.at[direction, hop, 0], az_sem.at[direction, hop, 1]),
            (o, right if direction == 0 else left),
        )

    def ap_copy(chip, at_home):
        block = aall.at[chip * 2 + (core if at_home else 1 - core)]
        return remote(block, block, (ap_sem.at[chip, 0], ap_sem.at[chip, 1]), (o, pair))

    @pl.when(z < last)
    def _():
        az_copy(0, 0, z).start()

    @pl.when(z > 0)
    def _():
        az_copy(1, 0, z).start()

    own_acts.wait()
    ap_copy(z, True).start()
    own_grads.wait()

    def acts_hop(hop):
        @pl.when(z >= hop)
        def _():
            az_copy(0, hop - 1, z - hop).wait_recv()
            if hop < last:
                @pl.when(z < last)
                def _():
                    az_copy(0, hop, z - hop).start()

            ap_copy(z - hop, True).start()

        @pl.when(z + hop <= last)
        def _():
            az_copy(1, hop - 1, z + hop).wait_recv()
            if hop < last:
                @pl.when(z > 0)
                def _():
                    az_copy(1, hop, z + hop).start()

            ap_copy(z + hop, True).start()

    wide = act_res.shape[2] // 2
    first, second = (xo, yo), (yo, xo)

    def quarter(side, keep, n):
        a = x if side == 0 else y
        a = a if keep else 1 - a
        return n * 2 + a if side == 0 else a * 2 + n

    def ax(side, n):
        return ax_sem.at[side, n, 0], ax_sem.at[side, n, 1]

    def ax_first(side, n):
        return remote(
            asend.at[side, quarter(side, False, n)], arecv1.at[side, n], ax(side, n), (first[side], i)
        )

    def ax_second(side):
        q = second[side]
        return remote(asend.at[side, q], arecv2.at[side], ax(side, 2), (q, i))

    def ax_columns(q, side):
        return act_res.at[q, :, pl.ds(side * wide, wide)]

    def ax_back(side, q):
        return remote(ax_columns(q, side), ax_columns(q, side), ax(side, 3), (second[side], i))

    def ax_all(side, n, keep):
        q = quarter(side, keep, n)
        return remote(ax_columns(q, side), ax_columns(q, side), ax(side, 4 + n), (first[side], i))

    def act_product():
        in_basis.wait()
        for chip in range(nz):
            ap_copy(chip, False).wait_recv()
        blocks = aall.shape[0] // 4

        def one(q, carry):
            lhs = aall[pl.ds(q * blocks, blocks)].reshape(blocks * arows, -1)
            for side in range(2):
                value = jnp.dot(
                    lhs, bin_[:, side * wide : (side + 1) * wide], preferred_element_type=jnp.float32
                )
                apart[side, q] = value
                asend[side, q] = encode(value, a_bound)
            return carry

        lax.fori_loop(0, 4, one, 0)
        for side in range(2):
            for n in range(2):
                ax_first(side, n).start()

    def act_second():
        for side in range(2):
            for n in range(2):
                ax_first(side, n).wait_recv()
                q = quarter(side, True, n)
                apart[side, q] = apart[side, q] + decode(arecv1[side, n], a_bound)
            q = second[side]
            asend[side, q] = encode(apart[side, q], a_bound)
            ax_second(side).start()

    def act_third():
        for side in range(2):
            ax_second(side).wait_recv()
            total = apart[side, o] + decode(arecv2[side], a_bound)
            act_res[o, :, side * wide : (side + 1) * wide] = total.astype(jnp.bfloat16)
            ax_back(side, o).start()

    def act_fourth():
        for side in range(2):
            ax_back(side, second[side]).wait_recv()
            for n in range(2):
                ax_all(side, n, True).start()

    def slot_of(k):
        return jnp.where(k < per, 0, jnp.where(k < 3 * per, 1 + (k - per) % 2, 3))

    def tile_of(k):
        return jnp.where(k < per, k, jnp.where(k < 3 * per, (k - per) // 2, k - 3 * per))

    def block_of(k):
        slot = slot_of(k)
        return (y + slot // 2) % 2 * 2 + (x + slot % 2) % 2

    def pair_copy(k):
        return remote(psend.at[k], precv.at[k], (s_sem.at[0], p_sem.at[k]), (o, pair))

    def sum_copy(d, k):
        return remote(rsend.at[d, k], rrecv.at[d, k], (s_sem.at[1 + d], r_sem.at[d, k]), (o, right if d == 0 else left))

    def place(d, k):
        return res.at[
            core * per + tile_of(k), pl.ds(d * HALF, HALF), pl.ds(pl.multiple_of(block_of(k) * rows, rows), rows)
        ]

    def out_copy(d, k):
        ref = place(d, k)
        return remote(ref, ref, (s_sem.at[3 + d], f_sem.at[d, k]), (o, left if d == 0 else right))

    def share_copy(d, k):
        ref = place(d, k)
        return remote(ref, ref, (s_sem.at[5], q_sem.at[0]), (o, pair))

    def chunk(v):
        return jnp.where(v < per, v, v - GAP)

    def valid(v):
        return ((v >= 0) & (v < per)) | ((v >= per + GAP) & (v < count + GAP))

    def product(lhs, k, j, blocks):
        theirs = jnp.dot(lhs, bout[2 * j], preferred_element_type=jnp.float32)
        for n in range(blocks):
            psend[k + n] = encode(theirs[n * rows : (n + 1) * rows], g_bound)
            pair_copy(k + n).start()
        mine = jnp.dot(lhs, bout[2 * j + 1], preferred_element_type=jnp.float32)
        for n in range(blocks):
            own[k + n] = mine[n * rows : (n + 1) * rows]

    def step(t, carry):
        for hop in range(1, nz):
            pl.when(t == 2 * hop)(functools.partial(acts_hop, hop))

        u = t - GAP

        @pl.when(u == per)
        def _():
            g_x.wait_recv()
            g_xy.start()
            g_y.wait_recv()
            g_yx.start()

        @pl.when(u == 3 * per)
        def _():
            g_xy.wait_recv()
            g_yx.wait_recv()

        pl.when(u == per + 8)(act_product)
        pl.when(u == 3 * per)(act_second)
        pl.when(u == 3 * per + 4)(act_third)
        pl.when(u == 4 * per)(act_fourth)

        @pl.when(t < per)
        def _():
            basis_copy(2 * t).wait()
            basis_copy(2 * t + 1).wait()
            product(gall[0], t, t, 1)

        @pl.when((u >= per) & (u < 3 * per) & ((u - per) % 2 == 0))
        def _():
            product(gall[1:3].reshape(2 * rows, -1), u, (u - per) // 2, 2)

        @pl.when((u >= 3 * per) & (u < count))
        def _():
            product(gall[3], u, u - 3 * per, 1)

        v = t - 1

        @pl.when(valid(v))
        def _():
            k = chunk(v)
            pair_copy(k).wait_recv()
            own[k] = own[k] + decode(precv[k], g_bound)

        for d in range(2):
            hops = z if d == 0 else last - z
            v = t - 1 - LAG * hops

            @pl.when(valid(v))
            def _(d=d, hops=hops, v=v):
                k = chunk(v)
                cols = slice(d * HALF, (d + 1) * HALF)

                @pl.when(hops == 0)
                def _():
                    rsend[d, k] = encode(own[k, :, cols], g_bound)
                    sum_copy(d, k).start()

                @pl.when((hops > 0) & (hops < last))
                def _():
                    sum_copy(d, k).wait_recv()
                    rsend[d, k] = encode(own[k, :, cols] + decode(rrecv[d, k], g_bound), g_bound)
                    sum_copy(d, k).start()

                @pl.when(hops == last)
                def _():
                    sum_copy(d, k).wait_recv()
                    total = own[k, :, cols] + decode(rrecv[d, k], g_bound)
                    place(d, k)[...] = total.T.astype(jnp.bfloat16)
                    out_copy(d, k).start()
                    share_copy(d, k).start()

            v2 = t - 1 - LAG * last - LAG * (last - hops)

            @pl.when(valid(v2) & (hops < last))
            def _(d=d, hops=hops, v=v2):
                k = chunk(v)
                out_copy(d, k).wait_recv()

                @pl.when(hops > 0)
                def _():
                    out_copy(d, k).start()

                share_copy(d, k).start()

        return carry

    lax.fori_loop(0, count + GAP + 1 + 2 * LAG * last, step, 0)

    for side in range(2):
        for n in range(2):
            ax_all(side, n, False).wait_recv()
            ax_all(side, n, True).wait_send()
            ax_first(side, n).wait_send()
        ax_second(side).wait_send()
        ax_back(side, o).wait_send()
    for copy in (g_x, g_y, g_xy, g_yx):
        copy.wait_send()
    for chip in range(nz):
        ap_copy(chip, True).wait_send()
    for hop in range(last):
        @pl.when((z < last) & (z >= hop))
        def _(hop=hop):
            az_copy(0, hop, z - hop).wait_send()

        @pl.when((z > 0) & (z + hop <= last))
        def _(hop=hop):
            az_copy(1, hop, z + hop).wait_send()

    def whole(ref, send, recv=0):
        return remote(ref, ref, (s_sem.at[send], q_sem.at[recv]), (o, pair))

    whole(psend, 0).wait_send()
    for d in range(2):
        hops = z if d == 0 else last - z

        @pl.when(hops < last)
        def _(d=d):
            whole(rsend.at[d], 1 + d).wait_send()

        @pl.when(hops > 0)
        def _(d=d):
            whole(res.at[pl.ds(core * per, per), pl.ds(d * HALF, HALF), :], 3 + d).wait_send()

    whole(res.at[pl.ds(core * per, per)], 5).wait_send()
    whole(res.at[pl.ds((1 - core) * per, per)], 5).wait_recv()


def rotate(nz, grads, acts, basis_out, basis_in):
    rows, arows = grads.shape[0], acts.shape[0]
    depth, columns = basis_out.shape
    adepth, acolumns = basis_in.shape
    tiles = columns // TILE
    count = 4 * (tiles // 2)
    wide = acolumns // 2
    blocks = 2 * nz
    g_bound = GRADS_MAX * BASIS_OUT_MAX * depth * blocks * 1.02
    a_bound = ACTS_MAX * BASIS_IN_MAX * adepth * 4 * 1.02
    dma = pltpu.SemaphoreType.DMA
    any_spec = pl.BlockSpec(memory_space=pl.ANY)
    vmem_spec = pl.BlockSpec(memory_space=pltpu.VMEM)
    return pl.pallas_call(
        functools.partial(rotate_kernel, nz, g_bound, a_bound),
        out_shape=(
            jax.ShapeDtypeStruct((tiles, TILE, 4 * rows), jnp.bfloat16),
            jax.ShapeDtypeStruct((4, blocks * arows // 4, acolumns), jnp.bfloat16),
        ),
        in_specs=[any_spec] * 4,
        out_specs=(vmem_spec, vmem_spec),
        scratch_shapes=[
            pltpu.VMEM((4, rows, depth), jnp.bfloat16),
            pltpu.VMEM((tiles, depth, TILE), jnp.bfloat16),
            pltpu.VMEM((adepth, acolumns), jnp.bfloat16),
            pltpu.VMEM((count, rows, TILE), jnp.float32),
            pltpu.VMEM((count, rows, TILE), WIRE),
            pltpu.VMEM((count, rows, TILE), WIRE),
            pltpu.VMEM((2, count, rows, HALF), WIRE),
            pltpu.VMEM((2, count, rows, HALF), WIRE),
            pltpu.VMEM((blocks, arows, adepth), jnp.bfloat16),
            pltpu.VMEM((2, 4, rows, wide), jnp.float32),
            pltpu.VMEM((2, 4, rows, wide), WIRE),
            pltpu.VMEM((2, 2, rows, wide), WIRE),
            pltpu.VMEM((2, rows, wide), WIRE),
            dma((3,)),
            dma((tiles,)),
            dma((4, 2)),
            dma((count,)),
            dma((2, count)),
            dma((2, count)),
            dma((1,)),
            dma((6,)),
            dma((2, nz - 1, 2)),
            dma((nz, 2)),
            dma((2, 6, 2)),
        ],
        compiler_params=pltpu.CompilerParams(
            collective_id=0, has_side_effects=True, vmem_limit_bytes=62 * 1024 * 1024
        ),
        name="rotate",
    )(grads, acts, basis_out, basis_in)


def correct_kernel(examples, lengths, grad, act, old, out, masked):
    windows = act.shape[0] // CAP
    columns = act.shape[1]
    offsets = [jnp.int32(0)]
    for e in range(examples):
        offsets.append(offsets[e] + lengths[e])

    def window(e):
        return jnp.minimum(offsets[e] // CAP, windows - 1)

    @pl.when(pl.program_id(0) == 0)
    def _():
        rows = lax.broadcasted_iota(jnp.int32, (CAP, 1), 0)
        for e in range(examples):
            for n in range(2):
                at = jnp.minimum(window(e) + n, windows - 1)
                places = (window(e) + n) * CAP + rows
                block = act[pl.ds(pl.multiple_of(at * CAP, CAP), CAP), :]
                inside = (places >= offsets[e]) & (places < offsets[e + 1])
                masked[e, n] = jnp.where(inside, block, jnp.zeros_like(block))

    scale = 0.2 / examples
    width = min(columns, TILE)
    for e in range(examples):
        first = window(e)

        def add(parts, e=e, first=first):
            lhs = [grad[:, pl.ds(pl.multiple_of((first + n) * CAP, CAP), CAP)] for n in range(parts)]
            for c in range(0, columns, width):
                cols = slice(c, c + width)
                projected = jnp.dot(lhs[0], masked[e, 0, :, cols], preferred_element_type=jnp.float32)
                if parts == 2:
                    projected += jnp.dot(lhs[1], masked[e, 1, :, cols], preferred_element_type=jnp.float32)
                base = 0.8 * old[:, cols] if e == 0 else out[:, cols]
                out[:, cols] = base + scale * (projected * projected)

        crosses = offsets[e + 1] > (first + 1) * CAP
        pl.when(crosses)(functools.partial(add, 2))
        pl.when(jnp.logical_not(crosses))(functools.partial(add, 1))


def correct(grad, act, old, lengths):
    total, tokens = grad.shape
    columns = act.shape[1]
    examples = lengths.shape[0]
    height = next(n for n in (512, 448, 256, 128) if total % n == 0)
    return pl.pallas_call(
        functools.partial(correct_kernel, examples),
        out_shape=jax.ShapeDtypeStruct(old.shape, jnp.float32),
        grid_spec=pltpu.PrefetchScalarGridSpec(
            num_scalar_prefetch=1,
            grid=(total // height,),
            in_specs=[
                pl.BlockSpec((height, tokens), lambda n, _: (n, 0)),
                pl.BlockSpec((tokens, columns), lambda n, _: (0, 0)),
                pl.BlockSpec((height, columns), lambda n, _: (n, 0)),
            ],
            out_specs=pl.BlockSpec((height, columns), lambda n, _: (n, 0)),
            scratch_shapes=[pltpu.VMEM((examples, 2, CAP, columns), jnp.bfloat16)],
        ),
        compiler_params=pltpu.CompilerParams(vmem_limit_bytes=62 * 1024 * 1024),
        name="correct",
    )(lengths, grad, act, old)


def gather_rotations(grads, acts, basis_out, basis_in):
    gathered = lax.all_gather(grads, "out", axis=0, tiled=True)
    scattered = lax.psum_scatter(
        lax.dot_general(basis_out, gathered, (((0,), (1,)), ((), ())), preferred_element_type=jnp.float32), "inp", scatter_dimension=0, tiled=True
    )
    grad_rot = lax.all_gather(scattered.astype(jnp.bfloat16), "inp", axis=0, tiled=True)
    gathered_acts = lax.all_gather(acts, "inp", axis=0, tiled=True)
    act_scattered = lax.psum_scatter(
        jnp.dot(gathered_acts, basis_in, preferred_element_type=jnp.float32), "out", scatter_dimension=0, tiled=True
    )
    act_rot = lax.all_gather(act_scattered.astype(jnp.bfloat16), "out", axis=0, tiled=True)
    return grad_rot, act_rot


def body(outs, nz, grads, acts, basis_out, basis_in, old_correction, lengths):
    if outs == 4:
        grad, act = rotate(nz, grads, acts, basis_out, basis_in)
        grad = grad.reshape(-1, grad.shape[-1])
        act = act.reshape(-1, act.shape[-1])
    else:
        grad, act = gather_rotations(grads, acts, basis_out, basis_in)
    return correct(grad, act, old_correction, lengths)


def solution(mesh):
    in_specs = (
        P("out", "inp"),
        P("inp", "out"),
        P("inp", "out"),
        P("out", "inp"),
        P("out", "inp"),
        P(),
    )
    run = functools.partial(body, mesh.shape["out"], mesh.shape["inp"] // 2)
    return jax.shard_map(run, mesh=mesh, in_specs=in_specs, out_specs=P("out", "inp"), check_vma=False)
```
